32 devices in a mesh: dp: 8 (over z, y), blk: 4 (over x, core).
Axes of the slice: x: 2, y: 2, z: 4, core: 2. Of those that a mesh axis runs over, the one named last changes fastest.
Arguments:
- features: bfloat16 [4096, 440], P('dp'), may hold values from -6 to 6
- residual: float32 [4096, 147], P(('dp', 'blk')), may hold values from -6 to 6
- block_weights: float32 [2, 2048, 147], P(None, ('dp', 'blk')), may hold values from -6 to 6
- block_inverse: float32 [2, 2048, 2048], P(None, None, ('dp', 'blk')), as said below
- block_columns: int32 [2, 2048], replicated, may hold values from 0 to 4095, as said below
Outputs:
- residual_out: float32 [4096, 147], P(('dp', 'blk'))
- weights_out: float32 [2, 2048, 147], P(None, ('dp', 'blk'))
The draws below stay inside these ranges and needn't reach their ends.
Inputs may be any that keep to these rules, and one draw needn't show every extreme that they name: `block_columns`: every frame number appears at most once over both blocks. `block_inverse`: each block's matrix is symmetric and positive definite.
All inputs are finite; a program needn't handle non-finite values.
Results may differ from the reference program's by a relative error of at most 0.011.
Values may be sent and summed in bfloat16 or wider, within the bound.
A program may use at most 64 MiB of HBM per device.

```python
import jax
import jax.numpy as jnp
from jax import lax

D = 440
CLASSES = 147
COLS = 2048
STEPS = 2
ROWS_DEV = 512
ROWS = 4096
N_DP = 8


def draw_block_columns(key, part):
    order = jax.random.permutation(key, ROWS)
    return order[:STEPS * COLS].reshape(STEPS, COLS).astype(jnp.int32)


def draw_block_inverse(key, part):
    key_off = jax.random.fold_in(key, 11)
    key_diag = jax.random.fold_in(key, 12)
    raw = jax.random.normal(key_off, (STEPS, COLS, COLS), jnp.float32) * (0.2 / COLS ** 0.5)
    symmetric = (raw + jnp.swapaxes(raw, 1, 2)) * 2.0 ** (-0.5)
    diagonal = jax.random.uniform(key_diag, (STEPS, COLS), jnp.float32, 0.5, 2.0)
    positions = jnp.arange(COLS)
    identity = (positions[:, None] == positions[None, :]).astype(jnp.float32)
    matrix = symmetric + identity[None, :, :] * diagonal[:, :, None]
    return matrix


def block_levels(own_key, extent, split, least, high):
    loudness, own = 1.0, jax.random.fold_in(own_key, 6)
    for position, parts in split:
        steps = jnp.exp(jax.random.uniform(jax.random.fold_in(own, position), (parts,), jnp.float32, least / len(split), high / len(split)))
        loudness = loudness * jnp.repeat(steps, extent[position] // parts).reshape([-1 if axis == position else 1 for axis in range(len(extent))])
    return loudness


def bell_draw(rng, shape, scale, bound, cuts=(), held_as=jnp.bfloat16):
    loudness = block_levels(rng, shape, cuts, -0.22, 0.18) if cuts else 1.0
    result = jax.random.normal(rng, shape, jnp.float32) * scale * loudness
    return jnp.minimum(jnp.maximum(result, -bound), bound).astype(held_as)


def setup_inputs(seed: int = 0) -> dict:
    streams_of = jax.random.split(jax.random.key(seed), 6)
    return {
        "features": bell_draw(streams_of[0], (ROWS, D), 1.0, 6.0, ((0, 8),)),
        "residual": bell_draw(streams_of[1], (ROWS, CLASSES), 1.0, 6.0, ((0, 32),), jnp.float32),
        "block_weights": bell_draw(streams_of[2], (STEPS, COLS, CLASSES), 1.0, 6.0, ((1, 32),), jnp.float32),
        "block_inverse": draw_block_inverse(jax.random.fold_in(streams_of[5], 71), 0),
        "block_columns": draw_block_columns(jax.random.fold_in(streams_of[5], 71), 0),
    }


RIDGE = 0.3


def kernel_block(frames, centers, center_sq, gamma_rate):
    cross = jnp.dot(frames, centers.T, preferred_element_type=jnp.float32)
    frame_f = frames.astype(jnp.float32)
    frame_sq = jnp.sum(frame_f * frame_f, axis=1)
    return jnp.exp(-gamma_rate * (frame_sq[:, None] + center_sq[None, :] - 2.0 * cross)).astype(jnp.bfloat16)


def reference(features, residual, block_weights, block_inverse, block_columns):
    gamma_rate = 4.0 / D
    feat_blocks = features.reshape(N_DP, ROWS_DEV, D)
    current = residual
    results = []
    for section in range(STEPS):
        columns = block_columns[section]
        centers = jnp.take(features, columns, axis=0)
        center_f = centers.astype(jnp.float32)
        center_sq = jnp.sum(center_f * center_f, axis=1)
        res_blocks = current.reshape(N_DP, ROWS_DEV, CLASSES)

        def grad_part(running, packed):
            frames, res_rows = packed
            kernel = kernel_block(frames, centers, center_sq, gamma_rate)
            term = lax.dot_general(kernel, res_rows.astype(jnp.bfloat16), (((0,), (0,)), ((), ())), preferred_element_type=jnp.float32)
            return running + term, None

        running, _ = lax.scan(grad_part, jnp.zeros((COLS, CLASSES), jnp.float32), (feat_blocks, res_blocks))
        gradient = running - RIDGE * block_weights[section]
        change = jnp.dot(block_inverse[section], gradient, precision=lax.Precision.HIGHEST, preferred_element_type=jnp.float32)
        results.append(block_weights[section] + change)
        change_low = change.astype(jnp.bfloat16)

        def update(packed):
            frames, res_rows = packed
            kernel = kernel_block(frames, centers, center_sq, gamma_rate)
            return res_rows - jnp.dot(kernel, change_low, preferred_element_type=jnp.float32)

        current = lax.map(update, (feat_blocks, res_blocks)).reshape(ROWS, CLASSES)
    return (current, jnp.stack(results))
```

```python
import functools

import jax
import jax.numpy as jnp
from jax import lax
from jax.experimental import pallas as pl
from jax.experimental.pallas import tpu as pltpu
from jax.sharding import PartitionSpec as P

RIDGE = 0.3
MESH = pl.DeviceIdType.MESH
F32 = jnp.float32
BF16 = jnp.bfloat16
FEAT, CUR0, GRAD0, CHANGE0, CUR1, GRAD1, CHANGE1 = range(7)
DIRECT, ACROSS, BESIDE, LAST = range(4)


def nt_dot(a, b):
    return lax.dot_general(a, b, (((1,), (1,)), ((), ())), preferred_element_type=F32)


def nn_dot(a, b):
    return jnp.dot(a, b, preferred_element_type=F32)


def fused_kernel(
    n,
    feat_ref,
    res_ref,
    weights_ref,
    inv_ref,
    own_ref,
    cols_ref,
    res_out,
    weights_out,
    feat_all,
    cur_all,
    grad_all,
    change_all,
    inv_parts,
    kern,
    kcol,
    send_sem,
    recv_sem,
):
    d, b = lax.axis_index("dp"), lax.axis_index("blk")
    groups = 4
    side = b + 1 - 2 * (b % 2)
    across = (b + 2) % 4
    beyond = (side + 2) % 4
    shard, width = feat_ref.shape
    rows = shard // groups
    own = weights_ref.shape[1]
    cols = cols_ref.shape[1]
    total = n * shard
    rate = 4.0 / width
    buffers = {
        FEAT: (feat_all, rows),
        CUR0: (cur_all.at[0], rows),
        CUR1: (cur_all.at[1], rows),
        GRAD0: (grad_all.at[0], own),
        GRAD1: (grad_all.at[1], own),
        CHANGE0: (change_all.at[0], own),
        CHANGE1: (change_all.at[1], own),
    }

    def block(which, source_d, source_b):
        buf, size = buffers[which]
        return buf.at[pl.ds(pl.multiple_of((source_d * groups + source_b) * size, size), size)]

    def remote(which, stage, ref, send_k, recv_k, to_d, to_b):
        return pltpu.make_async_remote_copy(
            src_ref=ref,
            dst_ref=ref,
            send_sem=send_sem.at[which, stage, send_k],
            recv_sem=recv_sem.at[which, stage, recv_k],
            device_id={"dp": to_d, "blk": to_b},
            device_id_type=MESH,
        )

    def direct(which, k):
        return remote(which, DIRECT, block(which, d, b), k, n - k, (d + k) % n, b)

    def arrival(which, stage, k):
        source = {DIRECT: b, ACROSS: across, BESIDE: side, LAST: beyond}[stage]
        return remote(which, stage, block(which, (d + k) % n, source), k, k, d, side)

    def pass_across(which, k):
        return remote(which, ACROSS, block(which, (d + k) % n, b), k, k, d, across)

    def pass_beside(which, k):
        return remote(which, BESIDE, block(which, (d + k) % n, b), k, k, d, side)

    def pass_last(which, k):
        return remote(which, LAST, block(which, (d + k) % n, across), k, k, d, side)

    def loop(first, last, body):
        lax.fori_loop(first, last, lambda k, c: (body(k), c)[1], 0)

    def begin(which):
        loop(1, n, lambda k: direct(which, k).start())
        if which != FEAT:
            pass_across(which, 0).start()
            pass_beside(which, 0).start()

    def forward(which):
        def step(k):
            arrival(which, DIRECT, k).wait_recv()
            pass_across(which, k).start()
            pass_beside(which, k).start()

        loop(1, n, step)

    def forward_last(which):
        def step(k):
            arrival(which, ACROSS, k).wait_recv()
            pass_last(which, k).start()

        loop(1 if which == FEAT else 0, n, step)

    def finish(which):
        def step(k):
            arrival(which, BESIDE, k).wait_recv()
            arrival(which, LAST, k).wait_recv()

        loop(1 if which == FEAT else 0, n, step)

    def drain(which):
        loop(1, n, lambda k: direct(which, k).wait_send())

        def step(k):
            pass_across(which, k).wait_send()
            pass_beside(which, k).wait_send()
            pass_last(which, k).wait_send()

        loop(1 if which == FEAT else 0, n, step)

    def own_rows(size):
        return pl.ds(pl.multiple_of((d * groups + b) * size, size), size)

    mine = pl.ds(pl.multiple_of(b * rows, rows), rows)
    feat_all[pl.ds(pl.multiple_of(d * shard, shard), shard), :] = feat_ref[...]
    cur_all[0, own_rows(rows), :] = res_ref[...].astype(BF16)

    barrier = pltpu.get_barrier_semaphore()
    for k in range(1, n):
        pl.semaphore_signal(
            barrier, inc=1, device_id={"dp": (d + k) % n, "blk": b}, device_id_type=MESH
        )
    for peer in (side, across):
        pl.semaphore_signal(barrier, inc=1, device_id={"dp": d, "blk": peer}, device_id_type=MESH)
    pl.semaphore_wait(barrier, n + 1)

    begin(FEAT)
    begin(CUR0)

    both = jnp.concatenate([inv_ref[0], inv_ref[1]], axis=1).T
    high = both.astype(BF16)
    rest = both - high.astype(F32)
    middle = rest.astype(BF16)
    low = (rest - middle.astype(F32)).astype(BF16)
    for s in range(2):
        part = slice(s * own, (s + 1) * own)
        inv_parts[s] = jnp.concatenate([high[part], middle[part], low[part]], axis=0)

    forward(FEAT)
    forward(CUR0)
    forward_last(FEAT)
    forward_last(CUR0)
    finish(FEAT)

    def pick(c, acc):
        frames = lax.broadcasted_iota(jnp.int32, (2 * own, shard), 1) + c * shard
        hot = jnp.where(frames == own_ref[...], 1.0, 0.0).astype(BF16)
        at = pl.ds(pl.multiple_of(c * shard, shard), shard)
        return acc + nn_dot(hot, feat_all[at, :])

    centers = lax.fori_loop(0, n, pick, jnp.zeros((2 * own, width), F32))
    left_f = jnp.concatenate([centers, feat_ref[mine, :].astype(F32)], axis=0)
    left = left_f.astype(BF16)
    left_sq = jnp.sum(left_f * left_f, axis=1, keepdims=True)
    ones = jnp.ones((16, width), BF16)

    def fill(c):
        at = pl.ds(pl.multiple_of(c * shard, shard), shard)
        right = feat_all[at, :]
        right_f = right.astype(F32)
        square = right_f * right_f
        square_high = square.astype(BF16)
        square_low = (square - square_high.astype(F32)).astype(BF16)
        right_sq = (nt_dot(ones, square_high) + nt_dot(ones, square_low))[0:1, :]
        cross = nt_dot(left, right)
        kern[:, at] = jnp.exp(-rate * (left_sq + right_sq - 2.0 * cross)).astype(BF16)

    loop(0, n, fill)

    def spread(s):
        tile = 512

        def step(c):
            at = pl.ds(pl.multiple_of(c * tile, tile), tile)
            wanted = cols_ref[pl.ds(s, 1), at]

            def inner(f, acc):
                frames = lax.broadcasted_iota(jnp.int32, (shard, tile), 0) + f * shard
                hot = jnp.where(frames == wanted, 1.0, 0.0).astype(BF16)
                here = pl.ds(pl.multiple_of(f * shard, shard), shard)
                return acc + nn_dot(kern[2 * own : 2 * own + rows, here], hot)

            kcol[s, :, at] = lax.fori_loop(0, n, inner, jnp.zeros((rows, tile), F32)).astype(BF16)

        loop(0, cols // tile, step)

    current = res_ref[...]
    finish(CUR0)
    for s, cur, grad, change in ((0, CUR0, GRAD0, CHANGE0), (1, CUR1, GRAD1, CHANGE1)):
        gradient = nn_dot(kern[s * own : (s + 1) * own, :], cur_all[s]) - RIDGE * weights_ref[s]
        grad_all[s, own_rows(own), :] = gradient.astype(BF16)
        begin(grad)
        if s == 0:
            spread(0)
        forward(grad)
        forward_last(grad)
        finish(grad)
        parts = nn_dot(inv_parts[s], grad_all[s])
        delta = parts[0:own] + (parts[own : 2 * own] + parts[2 * own : 3 * own])
        change_all[s, own_rows(own), :] = delta.astype(BF16)
        begin(change)
        weights_out[s] = weights_ref[s] + delta
        if s == 0:
            spread(1)
        forward(change)
        forward_last(change)
        finish(change)
        current = current - nn_dot(kcol[s], change_all[s])
        if s == 0:
            cur_all[1, own_rows(rows), :] = current.astype(BF16)
            begin(CUR1)
            forward(CUR1)
            forward_last(CUR1)
            finish(CUR1)
    res_out[...] = current
    for which in range(7):
        drain(which)


def fused(features, residual, block_weights, block_inverse, block_columns):
    n = lax.axis_size("dp")
    groups = lax.axis_size("blk")
    shard, width = features.shape
    rows, classes = residual.shape
    own = block_weights.shape[1]
    cols = block_columns.shape[1]
    place = lax.axis_index("dp") * groups + lax.axis_index("blk")
    own_columns = lax.dynamic_slice_in_dim(block_columns, place * own, own, 1).reshape(2 * own, 1)
    vmem = pl.BlockSpec(memory_space=pltpu.VMEM)
    return pl.pallas_call(
        functools.partial(fused_kernel, n),
        out_shape=(
            jax.ShapeDtypeStruct(residual.shape, F32),
            jax.ShapeDtypeStruct(block_weights.shape, F32),
        ),
        in_specs=[vmem] * 6,
        out_specs=(vmem, vmem),
        scratch_shapes=[
            pltpu.VMEM((n * shard, width), BF16),
            pltpu.VMEM((2, n * shard, classes), BF16),
            pltpu.VMEM((2, cols, classes), BF16),
            pltpu.VMEM((2, cols, classes), BF16),
            pltpu.VMEM((2, 3 * own, cols), BF16),
            pltpu.VMEM((2 * own + rows, n * shard), BF16),
            pltpu.VMEM((2, rows, cols), BF16),
            pltpu.SemaphoreType.DMA((7, 4, n)),
            pltpu.SemaphoreType.DMA((7, 4, n)),
        ],
        compiler_params=pltpu.CompilerParams(
            collective_id=0, has_side_effects=True, vmem_limit_bytes=48 * 2**20
        ),
    )(features, residual, block_weights, block_inverse, own_columns, block_columns)


def fits(features, residual, block_weights, block_columns):
    n, groups = lax.axis_size("dp"), lax.axis_size("blk")
    shard, width = features.shape
    own = block_weights.shape[1]
    return (
        groups == 4
        and block_columns.shape[0] == 2
        and own == 64
        and residual.shape[0] == 128
        and n * shard * (width + 512) <= 6 * 2**20
    )


def on_device(features, residual, block_weights, block_inverse, block_columns):
    if fits(features, residual, block_weights, block_columns):
        return fused(features, residual, block_weights, block_inverse, block_columns)
    data_count = lax.axis_size("dp")
    block_count = lax.axis_size("blk")
    data_index = lax.axis_index("dp")
    block_index = lax.axis_index("blk")
    row_count, width = features.shape
    own_count = block_weights.shape[1]
    column_count = block_columns.shape[1]
    piece_count = data_count * own_count
    gamma_rate = 4.0 / width
    frame_f = features.astype(jnp.float32)
    frame_sq = jnp.sum(frame_f * frame_f, axis=1)
    current = residual
    results = []
    for section in range(block_columns.shape[0]):
        layout = block_columns[section].reshape(data_count, block_count, own_count)
        chosen = lax.dynamic_index_in_dim(layout, block_index, 1, keepdims=False).reshape(
            piece_count
        )
        local_rows = chosen - data_index * row_count
        inside = (local_rows >= 0) & (local_rows < row_count)
        picked = jnp.take(features, jnp.clip(local_rows, 0, row_count - 1), axis=0).astype(
            jnp.float32
        )
        contrib = jnp.where(inside[:, None], picked, jnp.zeros_like(picked))
        centers = lax.psum(contrib, "dp")
        center_sq = jnp.sum(centers * centers, axis=1)
        cross = lax.dot_general(
            features,
            centers.astype(jnp.bfloat16),
            (((1,), (1,)), ((), ())),
            preferred_element_type=jnp.float32,
        )
        kernel = jnp.exp(
            -gamma_rate * (frame_sq[:, None] + center_sq[None, :] - 2.0 * cross)
        ).astype(jnp.bfloat16)
        partial_value = lax.dot_general(
            kernel,
            lax.all_gather(current.astype(jnp.bfloat16), "blk", axis=0, tiled=True),
            (((0,), (0,)), ((), ())),
            preferred_element_type=jnp.float32,
        )
        weights_own = block_weights[section]
        own_part = (
            lax.dynamic_slice_in_dim(partial_value, data_index * own_count, own_count, 0)
            - RIDGE * weights_own
        )
        partial_value = lax.dynamic_update_slice_in_dim(
            partial_value, own_part, data_index * own_count, 0
        )
        grad_piece = lax.psum(partial_value, "dp")
        stacked = lax.all_gather(grad_piece.astype(jnp.bfloat16), "blk", axis=0, tiled=True).astype(
            grad_piece.dtype
        )
        inverse = block_inverse[section].reshape(data_count, block_count, own_count, own_count)
        inverse = jnp.transpose(inverse, (1, 0, 2, 3)).reshape(column_count, own_count)
        change = lax.dot_general(
            inverse,
            stacked,
            (((0,), (0,)), ((), ())),
            precision=lax.Precision.HIGHEST,
            preferred_element_type=jnp.float32,
        )
        results.append(weights_own + change)
        change_all = lax.all_gather(change.astype(jnp.bfloat16), "dp", axis=0, tiled=True)
        current = current - lax.psum_scatter(
            jnp.dot(kernel, change_all, preferred_element_type=jnp.float32).astype(jnp.bfloat16),
            "blk",
            scatter_dimension=0,
            tiled=True,
        ).astype(jnp.float32)
    return (current, jnp.stack(results))


def solution(mesh):
    placed = (
        P("dp", None),
        P(("dp", "blk"), None),
        P(None, ("dp", "blk"), None),
        P(None, None, ("dp", "blk")),
        P(),
    )
    return jax.shard_map(
        on_device,
        mesh=mesh,
        in_specs=placed,
        out_specs=(P(("dp", "blk"), None), P(None, ("dp", "blk"), None)),
        check_vma=False,
    )
```

```python
import functools

import jax
import jax.numpy as jnp
from jax import lax
from jax.experimental import pallas as pl
from jax.experimental.pallas import tpu as pltpu
from jax.sharding import PartitionSpec as P

RIDGE = 0.3
MESH = pl.DeviceIdType.MESH
F32 = jnp.float32
BF16 = jnp.bfloat16
FEAT, CUR0, GRAD0, CHANGE0, CUR1, GRAD1, CHANGE1 = range(7)
DIRECT, ACROSS, BESIDE, LAST = range(4)


def nt_dot(a, b):
    return lax.dot_general(a, b, (((1,), (1,)), ((), ())), preferred_element_type=F32)


def nn_dot(a, b):
    return jnp.dot(a, b, preferred_element_type=F32)


def fused_kernel(
    n,
    feat_ref,
    res_ref,
    weights_ref,
    inv_ref,
    own_ref,
    cols_ref,
    res_out,
    weights_out,
    feat_all,
    cur_all,
    grad_all,
    change_all,
    inv_parts,
    kern,
    kcol,
    res_pad,
    weights_pad,
    send_sem,
    recv_sem,
):
    d, b = lax.axis_index("dp"), lax.axis_index("blk")
    groups = 4
    side = b + 1 - 2 * (b % 2)
    across = (b + 2) % 4
    beyond = (side + 2) % 4
    width, shard = feat_ref.shape
    depth = feat_all.shape[1]
    rows = shard // groups
    own, classes = weights_ref.shape[1:]
    cols = cols_ref.shape[1]
    total = n * shard
    rate = 4.0 / width
    slot = d * groups + b
    buffers = {
        FEAT: feat_all,
        CUR0: cur_all.at[0],
        CUR1: cur_all.at[1],
        GRAD0: grad_all.at[0],
        GRAD1: grad_all.at[1],
        CHANGE0: change_all.at[0],
        CHANGE1: change_all.at[1],
    }

    def block(which, source_d, source_b):
        return buffers[which].at[source_d * groups + source_b]

    def remote(which, stage, ref, send_k, recv_k, to_d, to_b):
        return pltpu.make_async_remote_copy(
            src_ref=ref,
            dst_ref=ref,
            send_sem=send_sem.at[which, stage, send_k],
            recv_sem=recv_sem.at[which, stage, recv_k],
            device_id={"dp": to_d, "blk": to_b},
            device_id_type=MESH,
        )

    def direct(which, k):
        return remote(which, DIRECT, block(which, d, b), k, n - k, (d + k) % n, b)

    def arrival(which, stage, k):
        source = {DIRECT: b, ACROSS: across, BESIDE: side, LAST: beyond}[stage]
        return remote(which, stage, block(which, (d + k) % n, source), k, k, d, side)

    def pass_across(which, k):
        return remote(which, ACROSS, block(which, (d + k) % n, b), k, k, d, across)

    def pass_beside(which, k):
        return remote(which, BESIDE, block(which, (d + k) % n, b), k, k, d, side)

    def pass_last(which, k):
        return remote(which, LAST, block(which, (d + k) % n, across), k, k, d, side)

    def loop(first, last, body):
        lax.fori_loop(first, last, lambda k, c: (body(k), c)[1], 0)

    def begin(which):
        loop(1, n, lambda k: direct(which, k).start())
        if which != FEAT:
            pass_across(which, 0).start()
            pass_beside(which, 0).start()

    def forward(which):
        def step(k):
            arrival(which, DIRECT, k).wait_recv()
            pass_across(which, k).start()
            pass_beside(which, k).start()

        loop(1, n, step)

    def forward_last(which):
        def step(k):
            arrival(which, ACROSS, k).wait_recv()
            pass_last(which, k).start()

        loop(1 if which == FEAT else 0, n, step)

    def finish(which):
        def step(k):
            arrival(which, BESIDE, k).wait_recv()
            arrival(which, LAST, k).wait_recv()

        loop(1 if which == FEAT else 0, n, step)

    def drain(which):
        loop(1, n, lambda k: direct(which, k).wait_send())

        def step(k):
            pass_across(which, k).wait_send()
            pass_beside(which, k).wait_send()
            pass_last(which, k).wait_send()

        loop(1 if which == FEAT else 0, n, step)

    def pack(values):
        count = values.shape[0] // 4
        lane = lax.broadcasted_iota(jnp.int32, (values.shape[0], 128), 1)
        tail = jnp.where(lane < classes - 128, values[:, 128:], 0.0)
        folded = tail[0:count]
        for q in range(1, 4):
            folded = folded + pltpu.roll(tail[q * count : (q + 1) * count], 32 * q, 1)
        return jnp.concatenate([values[:, :128], folded], axis=0).astype(BF16)

    def unpack(packed):
        slots, size = packed.shape[0], packed.shape[1] * 4 // 5
        main = packed[:, :size, :].reshape(slots * size, 128)
        folded = packed[:, size:, :].astype(F32).reshape(slots * size // 4, 128)
        parts = [folded] + [pltpu.roll(folded, 128 - 32 * q, 1) for q in range(1, 4)]
        parts = [p.astype(BF16).reshape(slots, size // 4, 128) for p in parts]
        tail = jnp.concatenate(parts, axis=1).reshape(slots * size, 128)
        return jnp.concatenate([main, tail], axis=1)

    res_pad[...] = jnp.zeros_like(res_pad)
    res_pad[0:classes, :] = res_ref[...]
    weights_pad[...] = jnp.zeros_like(weights_pad)
    weights_pad[:, :, 0:classes] = weights_ref[...]
    current = res_pad[...].T
    filled = jnp.concatenate(
        [feat_ref[...].astype(F32), jnp.zeros((depth - width, shard), F32)], axis=0
    ).astype(BF16)
    for q in range(groups):
        feat_all[d * groups + q] = filled[:, q * rows : (q + 1) * rows]
    cur_all[0, slot] = pack(current)

    barrier = pltpu.get_barrier_semaphore()
    for k in range(1, n):
        pl.semaphore_signal(
            barrier, inc=1, device_id={"dp": (d + k) % n, "blk": b}, device_id_type=MESH
        )
    for peer in (side, across):
        pl.semaphore_signal(barrier, inc=1, device_id={"dp": d, "blk": peer}, device_id_type=MESH)
    pl.semaphore_wait(barrier, n + 1)

    begin(FEAT)
    begin(CUR0)

    both = inv_ref[...].reshape(2 * own, cols)
    high = both.astype(BF16)
    rest = both - high.astype(F32)
    middle = rest.astype(BF16)
    low = (rest - middle.astype(F32)).astype(BF16)
    for s in range(2):
        part = slice(s * own, (s + 1) * own)
        inv_parts[s] = jnp.concatenate([high[part], middle[part], low[part]], axis=0)

    def first_forward(k):
        for which in (FEAT, CUR0):
            arrival(which, DIRECT, k).wait_recv()
            pass_across(which, k).start()
            pass_beside(which, k).start()

    def first_last(k):
        for which in (FEAT, CUR0):
            arrival(which, ACROSS, k).wait_recv()
            pass_last(which, k).start()

    loop(1, n, first_forward)
    arrival(CUR0, ACROSS, 0).wait_recv()
    pass_last(CUR0, 0).start()
    loop(1, n, first_last)
    finish(FEAT)

    row = lax.broadcasted_iota(jnp.int32, (rows, rows), 0)
    lane = lax.broadcasted_iota(jnp.int32, (rows, rows), 1)
    same = jnp.where(row == lane, 1.0, 0.0).astype(BF16)
    frames_own = nt_dot(same, feat_all[slot])

    def pick(c, acc):
        for q in range(groups):
            frames = lax.broadcasted_iota(jnp.int32, (2 * own, rows), 1) + (c * groups + q) * rows
            hot = jnp.where(frames == own_ref[...], 1.0, 0.0).astype(BF16)
            acc = acc + nt_dot(hot, feat_all[c * groups + q])
        return acc

    centers = lax.fori_loop(0, n, pick, jnp.zeros((2 * own, depth), F32))
    left_f = jnp.concatenate([centers, frames_own], axis=0)
    left = left_f.astype(BF16)
    left_sq = jnp.sum(left_f * left_f, axis=1, keepdims=True)

    def fill(c):
        at = pl.ds(pl.multiple_of(c * shard, shard), shard)
        right = jnp.concatenate([feat_all[c * groups + q] for q in range(groups)], axis=1)
        right_f = right.astype(F32)
        right_sq = jnp.sum(right_f * right_f, axis=0, keepdims=True)
        cross = nn_dot(left, right)
        kern[:, at] = jnp.exp(-rate * (left_sq + right_sq - 2.0 * cross)).astype(BF16)

    loop(0, n, fill)

    tile = cols // 4

    def spread(s, c):
        at = pl.ds(c * tile, tile)
        wanted = cols_ref[s : s + 1, at]

        def inner(f, acc):
            frames = lax.broadcasted_iota(jnp.int32, (shard, tile), 0) + f * shard
            hot = jnp.where(frames == wanted, 1.0, 0.0).astype(BF16)
            here = pl.ds(pl.multiple_of(f * shard, shard), shard)
            return acc + nn_dot(kern[2 * own : 2 * own + rows, here], hot)

        kcol[s, :, at] = lax.fori_loop(0, n, inner, jnp.zeros((rows, tile), F32)).astype(BF16)

    def gather(which, early=None, late=None):
        begin(which)
        if early is not None:
            spread(*early)
        forward(which)
        if late is not None:
            spread(*late)
        forward_last(which)
        finish(which)

    finish(CUR0)
    for s, grad, change in ((0, GRAD0, CHANGE0), (1, GRAD1, CHANGE1)):
        gradient = nn_dot(kern[s * own : (s + 1) * own, :], unpack(cur_all[s]))
        gradient = gradient - RIDGE * weights_pad[s]
        grad_all[s, slot] = pack(gradient)
        if s == 0:
            gather(grad, (0, 0), (0, 1))
        else:
            gather(grad, (1, 2), (1, 3))
        parts = nn_dot(inv_parts[s], unpack(grad_all[s]))
        delta = parts[0:own] + (parts[own : 2 * own] + parts[2 * own : 3 * own])
        change_all[s, slot] = pack(delta)
        weights_out[s] = weights_ref[s] + delta[:, :classes]
        if s == 0:
            gather(change, (0, 2), (0, 3))
        else:
            gather(change)
        current = current - nn_dot(kcol[s], unpack(change_all[s]))
        if s == 0:
            cur_all[1, slot] = pack(current)
            gather(CUR1, (1, 0), (1, 1))
    res_out[...] = current.T[0:classes, :]
    for which in range(7):
        drain(which)


def fused(features, residual, block_weights, block_inverse, block_columns):
    n = lax.axis_size("dp")
    groups = lax.axis_size("blk")
    shard, width = features.shape
    rows, classes = residual.shape
    own = block_weights.shape[1]
    cols = block_columns.shape[1]
    slots = n * groups
    depth = (width + 15) // 16 * 16
    place = lax.axis_index("dp") * groups + lax.axis_index("blk")
    own_columns = lax.dynamic_slice_in_dim(block_columns, place * own, own, 1).reshape(2 * own, 1)
    vmem = pl.BlockSpec(memory_space=pltpu.VMEM)
    res, weights = pl.pallas_call(
        functools.partial(fused_kernel, n),
        out_shape=(
            jax.ShapeDtypeStruct((classes, rows), F32),
            jax.ShapeDtypeStruct(block_weights.shape, F32),
        ),
        in_specs=[vmem] * 6,
        out_specs=(vmem, vmem),
        scratch_shapes=[
            pltpu.VMEM((slots, depth, rows), BF16),
            pltpu.VMEM((2, slots, rows + rows // 4, 128), BF16),
            pltpu.VMEM((2, slots, own + own // 4, 128), BF16),
            pltpu.VMEM((2, slots, own + own // 4, 128), BF16),
            pltpu.VMEM((2, 3 * own, cols), BF16),
            pltpu.VMEM((2 * own + rows, n * shard), BF16),
            pltpu.VMEM((2, rows, cols), BF16),
            pltpu.VMEM((256, rows), F32),
            pltpu.VMEM((2, own, 256), F32),
            pltpu.SemaphoreType.DMA((7, 4, n)),
            pltpu.SemaphoreType.DMA((7, 4, n)),
        ],
        compiler_params=pltpu.CompilerParams(
            collective_id=0, has_side_effects=True, vmem_limit_bytes=48 * 2**20
        ),
    )(
        features.T,
        residual.T,
        block_weights,
        jnp.swapaxes(block_inverse, 1, 2),
        own_columns,
        block_columns,
    )
    return res.T, weights


def fits(features, residual, block_weights, block_columns):
    n, groups = lax.axis_size("dp"), lax.axis_size("blk")
    shard, width = features.shape
    own, classes = block_weights.shape[1:]
    return (
        groups == 4
        and block_columns.shape[0] == 2
        and own == 64
        and residual.shape[0] == 128
        and 128 < classes <= 160
        and width % 8 == 0
        and n * shard * (width + 512) <= 6 * 2**20
    )


def on_device(features, residual, block_weights, block_inverse, block_columns):
    if fits(features, residual, block_weights, block_columns):
        return fused(features, residual, block_weights, block_inverse, block_columns)
    data_count = lax.axis_size("dp")
    block_count = lax.axis_size("blk")
    data_index = lax.axis_index("dp")
    block_index = lax.axis_index("blk")
    row_count, width = features.shape
    own_count = block_weights.shape[1]
    column_count = block_columns.shape[1]
    piece_count = data_count * own_count
    gamma_rate = 4.0 / width
    frame_f = features.astype(jnp.float32)
    frame_sq = jnp.sum(frame_f * frame_f, axis=1)
    current = residual
    results = []
    for section in range(block_columns.shape[0]):
        layout = block_columns[section].reshape(data_count, block_count, own_count)
        chosen = lax.dynamic_index_in_dim(layout, block_index, 1, keepdims=False).reshape(
            piece_count
        )
        local_rows = chosen - data_index * row_count
        inside = (local_rows >= 0) & (local_rows < row_count)
        picked = jnp.take(features, jnp.clip(local_rows, 0, row_count - 1), axis=0).astype(
            jnp.float32
        )
        contrib = jnp.where(inside[:, None], picked, jnp.zeros_like(picked))
        centers = lax.psum(contrib, "dp")
        center_sq = jnp.sum(centers * centers, axis=1)
        cross = lax.dot_general(
            features,
            centers.astype(jnp.bfloat16),
            (((1,), (1,)), ((), ())),
            preferred_element_type=jnp.float32,
        )
        kernel = jnp.exp(
            -gamma_rate * (frame_sq[:, None] + center_sq[None, :] - 2.0 * cross)
        ).astype(jnp.bfloat16)
        partial_value = lax.dot_general(
            kernel,
            lax.all_gather(current.astype(jnp.bfloat16), "blk", axis=0, tiled=True),
            (((0,), (0,)), ((), ())),
            preferred_element_type=jnp.float32,
        )
        weights_own = block_weights[section]
        own_part = (
            lax.dynamic_slice_in_dim(partial_value, data_index * own_count, own_count, 0)
            - RIDGE * weights_own
        )
        partial_value = lax.dynamic_update_slice_in_dim(
            partial_value, own_part, data_index * own_count, 0
        )
        grad_piece = lax.psum(partial_value, "dp")
        stacked = lax.all_gather(grad_piece.astype(jnp.bfloat16), "blk", axis=0, tiled=True).astype(
            grad_piece.dtype
        )
        inverse = block_inverse[section].reshape(data_count, block_count, own_count, own_count)
        inverse = jnp.transpose(inverse, (1, 0, 2, 3)).reshape(column_count, own_count)
        change = lax.dot_general(
            inverse,
            stacked,
            (((0,), (0,)), ((), ())),
            precision=lax.Precision.HIGHEST,
            preferred_element_type=jnp.float32,
        )
        results.append(weights_own + change)
        change_all = lax.all_gather(change.astype(jnp.bfloat16), "dp", axis=0, tiled=True)
        current = current - lax.psum_scatter(
            jnp.dot(kernel, change_all, preferred_element_type=jnp.float32).astype(jnp.bfloat16),
            "blk",
            scatter_dimension=0,
            tiled=True,
        ).astype(jnp.float32)
    return (current, jnp.stack(results))


def solution(mesh):
    placed = (
        P("dp", None),
        P(("dp", "blk"), None),
        P(None, ("dp", "blk"), None),
        P(None, None, ("dp", "blk")),
        P(),
    )
    return jax.shard_map(
        on_device,
        mesh=mesh,
        in_specs=placed,
        out_specs=(P(("dp", "blk"), None), P(None, ("dp", "blk"), None)),
        check_vma=False,
    )
```

```python
import functools

import jax
import jax.numpy as jnp
from jax import lax
from jax.experimental import pallas as pl
from jax.experimental.pallas import tpu as pltpu
from jax.sharding import PartitionSpec as P

RIDGE = 0.3
MESH = pl.DeviceIdType.MESH
F32 = jnp.float32
BF16 = jnp.bfloat16
FEAT, CUR0, GRAD0, CHANGE0, CUR1, GRAD1, CHANGE1 = range(7)
DIRECT, ACROSS, BESIDE, LAST = range(4)


def nt_dot(a, b):
    return lax.dot_general(a, b, (((1,), (1,)), ((), ())), preferred_element_type=F32)


def nn_dot(a, b):
    return jnp.dot(a, b, preferred_element_type=F32)


def fused_kernel(
    n,
    feat_ref,
    res_ref,
    weights_ref,
    inv_ref,
    own_ref,
    cols_ref,
    res_out,
    weights_out,
    feat_all,
    cur_all,
    grad_all,
    change_all,
    inv_parts,
    kern,
    kcol,
    res_pad,
    weights_pad,
    send_sem,
    recv_sem,
):
    d, b = lax.axis_index("dp"), lax.axis_index("blk")
    groups = 4
    side = b + 1 - 2 * (b % 2)
    across = (b + 2) % 4
    beyond = (side + 2) % 4
    width, shard = feat_ref.shape
    depth = feat_all.shape[1]
    rows = shard // groups
    own, classes = weights_ref.shape[1:]
    cols = cols_ref.shape[1]
    total = n * shard
    rate = 4.0 / width
    slot = b * n + d
    half = n // 2
    near = d // half
    buffers = {
        FEAT: feat_all,
        CUR0: cur_all.at[0],
        CUR1: cur_all.at[1],
        GRAD0: grad_all.at[0],
        GRAD1: grad_all.at[1],
        CHANGE0: change_all.at[0],
        CHANGE1: change_all.at[1],
    }

    def block(which, source_d, source_b):
        return buffers[which].at[source_b * n + source_d]

    def remote(which, stage, ref, send_k, recv_k, to_d, to_b):
        return pltpu.make_async_remote_copy(
            src_ref=ref,
            dst_ref=ref,
            send_sem=send_sem.at[which, stage, send_k],
            recv_sem=recv_sem.at[which, stage, recv_k],
            device_id={"dp": to_d, "blk": to_b},
            device_id_type=MESH,
        )

    def direct(which, k):
        return remote(which, DIRECT, block(which, d, b), k, n - k, (d + k) % n, b)

    def arrival(which, stage, k):
        source = {DIRECT: b, ACROSS: across, BESIDE: side, LAST: beyond}[stage]
        return remote(which, stage, block(which, (d + k) % n, source), k, k, d, side)

    def pass_across(which, k):
        return remote(which, ACROSS, block(which, (d + k) % n, b), k, k, d, across)

    def pass_beside(which, k):
        return remote(which, BESIDE, block(which, (d + k) % n, b), k, k, d, side)

    def pass_last(which, k):
        return remote(which, LAST, block(which, (d + k) % n, across), k, k, d, side)

    def loop(first, last, body):
        lax.fori_loop(first, last, lambda k, c: (body(k), c)[1], 0)

    def chunk(which, source_b, part):
        return buffers[which].at[pl.ds(source_b * n + part * half, half)]

    def push(which, to_d):
        return remote(which, DIRECT, block(which, d, b), to_d, d, to_d, b)

    def landed(which, from_d):
        return remote(which, DIRECT, block(which, from_d, b), from_d, from_d, d, side)

    def chunk_across(which, part):
        return remote(which, ACROSS, chunk(which, b, part), part, part, d, across)

    def chunk_beside(which, part):
        return remote(which, BESIDE, chunk(which, b, part), part, part, d, side)

    def chunk_last(which, part):
        return remote(which, LAST, chunk(which, across, part), part, part, d, side)

    def chunk_arrival(which, stage, part):
        source = {ACROSS: across, BESIDE: side, LAST: beyond}[stage]
        return remote(which, stage, chunk(which, source, part), part, part, d, side)

    def near_peer(k):
        return near * half + (d + k) % half

    def far_peer(k):
        return (1 - near) * half + (d + k) % half

    def begin(which):
        loop(1, half, lambda k: push(which, near_peer(k)).start())
        loop(0, half, lambda k: push(which, far_peer(k)).start())

    def forward(which):
        loop(1, half, lambda k: landed(which, near_peer(k)).wait_recv())
        chunk_across(which, near).start()
        chunk_beside(which, near).start()
        loop(0, half, lambda k: landed(which, far_peer(k)).wait_recv())
        chunk_across(which, 1 - near).start()
        chunk_beside(which, 1 - near).start()

    def forward_last(which):
        for part in (near, 1 - near):
            chunk_arrival(which, ACROSS, part).wait_recv()
            chunk_last(which, part).start()

    def finish(which):
        for stage in (BESIDE, LAST):
            for part in (near, 1 - near):
                chunk_arrival(which, stage, part).wait_recv()

    def drain(which):
        loop(1, half, lambda k: push(which, near_peer(k)).wait_send())
        loop(0, half, lambda k: push(which, far_peer(k)).wait_send())
        for part in (near, 1 - near):
            chunk_across(which, part).wait_send()
            chunk_beside(which, part).wait_send()
            chunk_last(which, part).wait_send()

    def pack(values):
        count = values.shape[0] // 4
        lane = lax.broadcasted_iota(jnp.int32, (values.shape[0], 128), 1)
        tail = jnp.where(lane < classes - 128, values[:, 128:], 0.0)
        folded = tail[0:count]
        for q in range(1, 4):
            folded = folded + pltpu.roll(tail[q * count : (q + 1) * count], 32 * q, 1)
        return jnp.concatenate([values[:, :128], folded], axis=0).astype(BF16)

    def unpack(packed):
        order = [packed[q * n + c][None] for c in range(n) for q in range(groups)]
        packed = jnp.concatenate(order, axis=0)
        slots, size = packed.shape[0], packed.shape[1] * 4 // 5
        main = packed[:, :size, :].reshape(slots * size, 128)
        folded = packed[:, size:, :].astype(F32).reshape(slots * size // 4, 128)
        parts = [folded] + [pltpu.roll(folded, 128 - 32 * q, 1) for q in range(1, 4)]
        parts = [p.astype(BF16).reshape(slots, size // 4, 128) for p in parts]
        tail = jnp.concatenate(parts, axis=1).reshape(slots * size, 128)
        return jnp.concatenate([main, tail], axis=1)

    res_pad[...] = jnp.zeros_like(res_pad)
    res_pad[0:classes, :] = res_ref[...]
    weights_pad[...] = jnp.zeros_like(weights_pad)
    weights_pad[:, :, 0:classes] = weights_ref[...]
    current = res_pad[...].T
    filled = jnp.concatenate(
        [feat_ref[...].astype(F32), jnp.zeros((depth - width, shard), F32)], axis=0
    ).astype(BF16)
    for q in range(groups):
        feat_all[q * n + d] = filled[:, q * rows : (q + 1) * rows]
    cur_all[0, slot] = pack(current)

    barrier = pltpu.get_barrier_semaphore()
    for k in range(1, n):
        pl.semaphore_signal(
            barrier, inc=1, device_id={"dp": (d + k) % n, "blk": b}, device_id_type=MESH
        )
    for peer in (side, across):
        pl.semaphore_signal(barrier, inc=1, device_id={"dp": d, "blk": peer}, device_id_type=MESH)
    pl.semaphore_wait(barrier, n + 1)

    loop(1, n, lambda k: direct(FEAT, k).start())
    begin(CUR0)

    both = inv_ref[...].reshape(2 * own, cols)
    high = both.astype(BF16)
    rest = both - high.astype(F32)
    middle = rest.astype(BF16)
    low = (rest - middle.astype(F32)).astype(BF16)
    for s in range(2):
        part = slice(s * own, (s + 1) * own)
        inv_parts[s] = jnp.concatenate([high[part], middle[part], low[part]], axis=0)

    def feat_forward(k):
        arrival(FEAT, DIRECT, k).wait_recv()
        pass_across(FEAT, k).start()
        pass_beside(FEAT, k).start()

    def feat_last(k):
        arrival(FEAT, ACROSS, k).wait_recv()
        pass_last(FEAT, k).start()

    def feat_finish(k):
        arrival(FEAT, BESIDE, k).wait_recv()
        arrival(FEAT, LAST, k).wait_recv()

    def feat_drain(k):
        direct(FEAT, k).wait_send()
        pass_across(FEAT, k).wait_send()
        pass_beside(FEAT, k).wait_send()
        pass_last(FEAT, k).wait_send()

    loop(1, n, feat_forward)
    forward(CUR0)
    loop(1, n, feat_last)
    forward_last(CUR0)
    loop(1, n, feat_finish)

    row = lax.broadcasted_iota(jnp.int32, (rows, rows), 0)
    lane = lax.broadcasted_iota(jnp.int32, (rows, rows), 1)
    same = jnp.where(row == lane, 1.0, 0.0).astype(BF16)
    frames_own = nt_dot(same, feat_all[slot])

    def pick(c, acc):
        for q in range(groups):
            frames = lax.broadcasted_iota(jnp.int32, (2 * own, rows), 1)
            wanted = own_ref[...] - (c * groups + q) * rows
            hot = jnp.where(frames == wanted, 1.0, 0.0).astype(BF16)
            acc = acc + nt_dot(hot, feat_all[q * n + c])
        return acc

    centers = lax.fori_loop(0, n, pick, jnp.zeros((2 * own, depth), F32))
    left_f = jnp.concatenate([centers, frames_own], axis=0)
    left = left_f.astype(BF16)
    left_sq = jnp.sum(left_f * left_f, axis=1, keepdims=True)

    def fill(c):
        at = pl.ds(pl.multiple_of(c * shard, shard), shard)
        right = jnp.concatenate([feat_all[q * n + c] for q in range(groups)], axis=1)
        right_f = right.astype(F32)
        right_sq = jnp.sum(right_f * right_f, axis=0, keepdims=True)
        cross = nn_dot(left, right)
        kern[:, at] = jnp.exp(-rate * (left_sq + right_sq - 2.0 * cross)).astype(BF16)

    loop(0, n, fill)

    tile = cols // 4

    def spread(s, c):
        at = pl.ds(c * tile, tile)
        wanted = cols_ref[s : s + 1, at]

        def inner(f, acc):
            frames = lax.broadcasted_iota(jnp.int32, (shard, tile), 0)
            hot = jnp.where(frames == wanted - f * shard, 1.0, 0.0).astype(BF16)
            here = pl.ds(pl.multiple_of(f * shard, shard), shard)
            return acc + nn_dot(kern[2 * own : 2 * own + rows, here], hot)

        kcol[s, :, at] = lax.fori_loop(0, n, inner, jnp.zeros((rows, tile), F32)).astype(BF16)

    def gather(which, early=None, late=None):
        begin(which)
        if early is not None:
            spread(*early)
        forward(which)
        if late is not None:
            spread(*late)
        forward_last(which)
        finish(which)

    finish(CUR0)
    for s, grad, change in ((0, GRAD0, CHANGE0), (1, GRAD1, CHANGE1)):
        gradient = nn_dot(kern[s * own : (s + 1) * own, :], unpack(cur_all[s]))
        gradient = gradient - RIDGE * weights_pad[s]
        grad_all[s, slot] = pack(gradient)
        if s == 0:
            gather(grad, (0, 0), (0, 1))
        else:
            gather(grad, (1, 2), (1, 3))
        parts = nn_dot(inv_parts[s], unpack(grad_all[s]))
        delta = parts[0:own] + (parts[own : 2 * own] + parts[2 * own : 3 * own])
        change_all[s, slot] = pack(delta)
        weights_out[s] = weights_ref[s] + delta[:, :classes]
        if s == 0:
            gather(change, (0, 2), (0, 3))
        else:
            gather(change)
        current = current - nn_dot(kcol[s], unpack(change_all[s]))
        if s == 0:
            cur_all[1, slot] = pack(current)
            gather(CUR1, (1, 0), (1, 1))
    res_out[...] = current.T[0:classes, :]
    loop(1, n, feat_drain)
    for which in range(1, 7):
        drain(which)


def fused(features, residual, block_weights, block_inverse, block_columns):
    n = lax.axis_size("dp")
    groups = lax.axis_size("blk")
    shard, width = features.shape
    rows, classes = residual.shape
    own = block_weights.shape[1]
    cols = block_columns.shape[1]
    slots = n * groups
    depth = (width + 15) // 16 * 16
    place = lax.axis_index("dp") * groups + lax.axis_index("blk")
    own_columns = lax.dynamic_slice_in_dim(block_columns, place * own, own, 1).reshape(2 * own, 1)
    vmem = pl.BlockSpec(memory_space=pltpu.VMEM)
    res, weights = pl.pallas_call(
        functools.partial(fused_kernel, n),
        out_shape=(
            jax.ShapeDtypeStruct((classes, rows), F32),
            jax.ShapeDtypeStruct(block_weights.shape, F32),
        ),
        in_specs=[vmem] * 6,
        out_specs=(vmem, vmem),
        scratch_shapes=[
            pltpu.VMEM((slots, depth, rows), BF16),
            pltpu.VMEM((2, slots, rows + rows // 4, 128), BF16),
            pltpu.VMEM((2, slots, own + own // 4, 128), BF16),
            pltpu.VMEM((2, slots, own + own // 4, 128), BF16),
            pltpu.VMEM((2, 3 * own, cols), BF16),
            pltpu.VMEM((2 * own + rows, n * shard), BF16),
            pltpu.VMEM((2, rows, cols), BF16),
            pltpu.VMEM((256, rows), F32),
            pltpu.VMEM((2, own, 256), F32),
            pltpu.SemaphoreType.DMA((7, 4, n)),
            pltpu.SemaphoreType.DMA((7, 4, n)),
        ],
        compiler_params=pltpu.CompilerParams(
            collective_id=0, has_side_effects=True, vmem_limit_bytes=48 * 2**20
        ),
    )(
        features.T,
        residual.T,
        block_weights,
        jnp.swapaxes(block_inverse, 1, 2),
        own_columns,
        block_columns,
    )
    return res.T, weights


def fits(features, residual, block_weights, block_columns):
    n, groups = lax.axis_size("dp"), lax.axis_size("blk")
    shard, width = features.shape
    own, classes = block_weights.shape[1:]
    return (
        groups == 4
        and block_columns.shape[0] == 2
        and own == 64
        and residual.shape[0] == 128
        and 128 < classes <= 160
        and width % 8 == 0
        and n == 8
        and n * shard * (width + 512) <= 6 * 2**20
    )


def on_device(features, residual, block_weights, block_inverse, block_columns):
    if fits(features, residual, block_weights, block_columns):
        return fused(features, residual, block_weights, block_inverse, block_columns)
    data_count = lax.axis_size("dp")
    block_count = lax.axis_size("blk")
    data_index = lax.axis_index("dp")
    block_index = lax.axis_index("blk")
    row_count, width = features.shape
    own_count = block_weights.shape[1]
    column_count = block_columns.shape[1]
    piece_count = data_count * own_count
    gamma_rate = 4.0 / width
    frame_f = features.astype(jnp.float32)
    frame_sq = jnp.sum(frame_f * frame_f, axis=1)
    current = residual
    results = []
    for section in range(block_columns.shape[0]):
        layout = block_columns[section].reshape(data_count, block_count, own_count)
        chosen = lax.dynamic_index_in_dim(layout, block_index, 1, keepdims=False).reshape(
            piece_count
        )
        local_rows = chosen - data_index * row_count
        inside = (local_rows >= 0) & (local_rows < row_count)
        picked = jnp.take(features, jnp.clip(local_rows, 0, row_count - 1), axis=0).astype(
            jnp.float32
        )
        contrib = jnp.where(inside[:, None], picked, jnp.zeros_like(picked))
        centers = lax.psum(contrib, "dp")
        center_sq = jnp.sum(centers * centers, axis=1)
        cross = lax.dot_general(
            features,
            centers.astype(jnp.bfloat16),
            (((1,), (1,)), ((), ())),
            preferred_element_type=jnp.float32,
        )
        kernel = jnp.exp(
            -gamma_rate * (frame_sq[:, None] + center_sq[None, :] - 2.0 * cross)
        ).astype(jnp.bfloat16)
        partial_value = lax.dot_general(
            kernel,
            lax.all_gather(current.astype(jnp.bfloat16), "blk", axis=0, tiled=True),
            (((0,), (0,)), ((), ())),
            preferred_element_type=jnp.float32,
        )
        weights_own = block_weights[section]
        own_part = (
            lax.dynamic_slice_in_dim(partial_value, data_index * own_count, own_count, 0)
            - RIDGE * weights_own
        )
        partial_value = lax.dynamic_update_slice_in_dim(
            partial_value, own_part, data_index * own_count, 0
        )
        grad_piece = lax.psum(partial_value, "dp")
        stacked = lax.all_gather(grad_piece.astype(jnp.bfloat16), "blk", axis=0, tiled=True).astype(
            grad_piece.dtype
        )
        inverse = block_inverse[section].reshape(data_count, block_count, own_count, own_count)
        inverse = jnp.transpose(inverse, (1, 0, 2, 3)).reshape(column_count, own_count)
        change = lax.dot_general(
            inverse,
            stacked,
            (((0,), (0,)), ((), ())),
            precision=lax.Precision.HIGHEST,
            preferred_element_type=jnp.float32,
        )
        results.append(weights_own + change)
        change_all = lax.all_gather(change.astype(jnp.bfloat16), "dp", axis=0, tiled=True)
        current = current - lax.psum_scatter(
            jnp.dot(kernel, change_all, preferred_element_type=jnp.float32).astype(jnp.bfloat16),
            "blk",
            scatter_dimension=0,
            tiled=True,
        ).astype(jnp.float32)
    return (current, jnp.stack(results))


def solution(mesh):
    placed = (
        P("dp", None),
        P(("dp", "blk"), None),
        P(None, ("dp", "blk"), None),
        P(None, None, ("dp", "blk")),
        P(),
    )
    return jax.shard_map(
        on_device,
        mesh=mesh,
        in_specs=placed,
        out_specs=(P(("dp", "blk"), None), P(None, ("dp", "blk"), None)),
        check_vma=False,
    )
```

```python
import functools

import jax
import jax.numpy as jnp
from jax import lax
from jax.experimental import pallas as pl
from jax.experimental.pallas import tpu as pltpu
from jax.sharding import PartitionSpec as P

RIDGE = 0.3
MESH = pl.DeviceIdType.MESH
F32 = jnp.float32
BF16 = jnp.bfloat16
FEAT, CUR0, GRAD0, CHANGE0, CUR1, GRAD1, CHANGE1 = range(7)
DIRECT, ACROSS, BESIDE, LAST = range(4)


def nt_dot(a, b):
    return lax.dot_general(a, b, (((1,), (1,)), ((), ())), preferred_element_type=F32)


def nn_dot(a, b):
    return jnp.dot(a, b, preferred_element_type=F32)


def fused_kernel(
    n,
    feat_ref,
    res_ref,
    weights_ref,
    inv_ref,
    own_ref,
    cols_ref,
    res_out,
    weights_out,
    feat_all,
    cur_all,
    grad_all,
    change_all,
    inv_parts,
    kern,
    kcol,
    res_pad,
    weights_pad,
    send_sem,
    recv_sem,
):
    d, b = lax.axis_index("dp"), lax.axis_index("blk")
    groups = 4
    side = b + 1 - 2 * (b % 2)
    across = (b + 2) % 4
    beyond = (side + 2) % 4
    width, shard = feat_ref.shape
    depth = feat_all.shape[1]
    rows = shard // groups
    own, classes = weights_ref.shape[1:]
    cols = cols_ref.shape[1]
    total = n * shard
    rate = 4.0 / width
    slot = b * n + d
    half = n // 2
    near = d // half
    buffers = {
        FEAT: feat_all,
        CUR0: cur_all.at[0],
        CUR1: cur_all.at[1],
        GRAD0: grad_all.at[0],
        GRAD1: grad_all.at[1],
        CHANGE0: change_all.at[0],
        CHANGE1: change_all.at[1],
    }

    def block(which, source_d, source_b):
        return buffers[which].at[source_b * n + source_d]

    def remote(which, stage, ref, send_k, recv_k, to_d, to_b):
        return pltpu.make_async_remote_copy(
            src_ref=ref,
            dst_ref=ref,
            send_sem=send_sem.at[which, stage, send_k],
            recv_sem=recv_sem.at[which, stage, recv_k],
            device_id={"dp": to_d, "blk": to_b},
            device_id_type=MESH,
        )

    def direct(which, k):
        return remote(which, DIRECT, block(which, d, b), k, n - k, (d + k) % n, b)

    def arrival(which, stage, k):
        source = {DIRECT: b, ACROSS: across, BESIDE: side, LAST: beyond}[stage]
        return remote(which, stage, block(which, (d + k) % n, source), k, k, d, side)

    def pass_across(which, k):
        return remote(which, ACROSS, block(which, (d + k) % n, b), k, k, d, across)

    def pass_beside(which, k):
        return remote(which, BESIDE, block(which, (d + k) % n, b), k, k, d, side)

    def pass_last(which, k):
        return remote(which, LAST, block(which, (d + k) % n, across), k, k, d, side)

    def loop(first, last, body):
        lax.fori_loop(first, last, lambda k, c: (body(k), c)[1], 0)

    def chunk(which, source_b, part):
        return buffers[which].at[pl.ds(source_b * n + part * half, half)]

    def push(which, to_d):
        return remote(which, DIRECT, block(which, d, b), to_d, d, to_d, b)

    def landed(which, from_d):
        return remote(which, DIRECT, block(which, from_d, b), from_d, from_d, d, side)

    def chunk_across(which, part):
        return remote(which, ACROSS, chunk(which, b, part), part, part, d, across)

    def chunk_beside(which, part):
        return remote(which, BESIDE, chunk(which, b, part), part, part, d, side)

    def chunk_last(which, part):
        return remote(which, LAST, chunk(which, across, part), part, part, d, side)

    def chunk_arrival(which, stage, part):
        source = {ACROSS: across, BESIDE: side, LAST: beyond}[stage]
        return remote(which, stage, chunk(which, source, part), part, part, d, side)

    def near_peer(k):
        return near * half + (d + k) % half

    def far_peer(k):
        return (1 - near) * half + (d + k) % half

    def begin(which):
        loop(1, half, lambda k: push(which, near_peer(k)).start())
        loop(0, half, lambda k: push(which, far_peer(k)).start())

    def forward(which):
        loop(1, half, lambda k: landed(which, near_peer(k)).wait_recv())
        chunk_across(which, near).start()
        chunk_beside(which, near).start()
        loop(0, half, lambda k: landed(which, far_peer(k)).wait_recv())
        chunk_across(which, 1 - near).start()
        chunk_beside(which, 1 - near).start()

    def forward_last(which):
        for part in (near, 1 - near):
            chunk_arrival(which, ACROSS, part).wait_recv()
            chunk_last(which, part).start()

    def finish(which):
        for stage in (BESIDE, LAST):
            for part in (near, 1 - near):
                chunk_arrival(which, stage, part).wait_recv()

    def drain(which):
        loop(1, half, lambda k: push(which, near_peer(k)).wait_send())
        loop(0, half, lambda k: push(which, far_peer(k)).wait_send())
        for part in (near, 1 - near):
            chunk_across(which, part).wait_send()
            chunk_beside(which, part).wait_send()
            chunk_last(which, part).wait_send()

    def pack(values):
        count = values.shape[0] // 4
        lane = lax.broadcasted_iota(jnp.int32, (values.shape[0], 128), 1)
        tail = jnp.where(lane < classes - 128, values[:, 128:], 0.0)
        folded = tail[0:count]
        for q in range(1, 4):
            folded = folded + pltpu.roll(tail[q * count : (q + 1) * count], 32 * q, 1)
        return jnp.concatenate([values[:, :128], folded], axis=0).astype(BF16)

    def unpack(packed):
        order = [packed[q * n + c][None] for c in range(n) for q in range(groups)]
        packed = jnp.concatenate(order, axis=0)
        slots, size = packed.shape[0], packed.shape[1] * 4 // 5
        main = packed[:, :size, :].reshape(slots * size, 128)
        folded = packed[:, size:, :].astype(F32).reshape(slots * size // 4, 128)
        parts = [folded] + [pltpu.roll(folded, 128 - 32 * q, 1) for q in range(1, 4)]
        parts = [p.astype(BF16).reshape(slots, size // 4, 128) for p in parts]
        tail = jnp.concatenate(parts, axis=1).reshape(slots * size, 128)
        return jnp.concatenate([main, tail], axis=1)

    res_pad[...] = jnp.zeros_like(res_pad)
    res_pad[0:classes, :] = res_ref[...]
    weights_pad[...] = jnp.zeros_like(weights_pad)
    weights_pad[:, :, 0:classes] = weights_ref[...]
    current = res_pad[...].T
    filled = jnp.concatenate(
        [feat_ref[...].astype(F32), jnp.zeros((depth - width, shard), F32)], axis=0
    ).astype(BF16)
    for q in range(groups):
        feat_all[q * n + d] = filled[:, q * rows : (q + 1) * rows]
    cur_all[0, slot] = pack(current)

    barrier = pltpu.get_barrier_semaphore()
    for k in range(1, n):
        pl.semaphore_signal(
            barrier, inc=1, device_id={"dp": (d + k) % n, "blk": b}, device_id_type=MESH
        )
    for peer in (side, across):
        pl.semaphore_signal(barrier, inc=1, device_id={"dp": d, "blk": peer}, device_id_type=MESH)
    pl.semaphore_wait(barrier, n + 1)

    loop(1, n, lambda k: direct(FEAT, k).start())
    begin(CUR0)

    both = inv_ref[...].reshape(2 * own, cols)
    high = both.astype(BF16)
    rest = both - high.astype(F32)
    middle = rest.astype(BF16)
    low = (rest - middle.astype(F32)).astype(BF16)
    for s in range(2):
        part = slice(s * own, (s + 1) * own)
        inv_parts[s] = jnp.concatenate([high[part], middle[part], low[part]], axis=0)

    def feat_forward(k):
        arrival(FEAT, DIRECT, k).wait_recv()
        pass_across(FEAT, k).start()
        pass_beside(FEAT, k).start()

    def feat_last(k):
        arrival(FEAT, ACROSS, k).wait_recv()
        pass_last(FEAT, k).start()

    def feat_finish(k):
        arrival(FEAT, BESIDE, k).wait_recv()
        arrival(FEAT, LAST, k).wait_recv()

    def feat_drain(k):
        direct(FEAT, k).wait_send()
        pass_across(FEAT, k).wait_send()
        pass_beside(FEAT, k).wait_send()
        pass_last(FEAT, k).wait_send()

    loop(1, n, feat_forward)
    forward(CUR0)
    loop(1, n, feat_last)
    forward_last(CUR0)
    loop(1, n, feat_finish)

    row = lax.broadcasted_iota(jnp.int32, (rows, rows), 0)
    lane = lax.broadcasted_iota(jnp.int32, (rows, rows), 1)
    same = jnp.where(row == lane, 1.0, 0.0).astype(BF16)
    frames_own = nt_dot(same, feat_all[slot])

    def pick(c, acc):
        for q in range(groups):
            frames = lax.broadcasted_iota(jnp.int32, (2 * own, rows), 1)
            wanted = own_ref[...] - (c * groups + q) * rows
            hot = jnp.where(frames == wanted, 1.0, 0.0).astype(BF16)
            acc = acc + nt_dot(hot, feat_all[q * n + c])
        return acc

    centers = lax.fori_loop(0, n, pick, jnp.zeros((2 * own, depth), F32))
    left_f = jnp.concatenate([centers, frames_own], axis=0)
    left = left_f.astype(BF16)
    left_sq = jnp.sum(left_f * left_f, axis=1, keepdims=True)

    def fill(c):
        at = pl.ds(pl.multiple_of(c * shard, shard), shard)
        right = jnp.concatenate([feat_all[q * n + c] for q in range(groups)], axis=1)
        right_f = right.astype(F32)
        right_sq = jnp.sum(right_f * right_f, axis=0, keepdims=True)
        cross = nn_dot(left, right)
        kern[:, at] = jnp.exp(-rate * (left_sq + right_sq - 2.0 * cross)).astype(BF16)

    loop(0, n, fill)

    tile = cols // 4

    def spread(s, c):
        at = pl.ds(c * tile, tile)
        wanted = cols_ref[s : s + 1, at]

        lines = lax.broadcasted_iota(jnp.int32, (256, tile), 0).astype(F32).astype(BF16)
        one, zero = jnp.ones((256, tile), BF16), jnp.zeros((256, tile), BF16)

        def inner(f, acc):
            hots = []
            for part in range(2 * shard // 256):
                local = wanted - (f * 2 * shard + part * 256)
                local = jnp.where((local >= 0) & (local < 256), local, -1)
                local = jnp.broadcast_to(local.astype(F32).astype(BF16), (256, tile))
                hots.append(jnp.where(lines == local, one, zero))
            hot = jnp.concatenate(hots, axis=0)
            here = pl.ds(pl.multiple_of(f * 2 * shard, 2 * shard), 2 * shard)
            return acc + nn_dot(kern[2 * own : 2 * own + rows, here], hot)

        kcol[s, :, at] = lax.fori_loop(0, n // 2, inner, jnp.zeros((rows, tile), F32)).astype(BF16)

    def gather(which, early=None, late=None):
        begin(which)
        if early is not None:
            spread(*early)
        forward(which)
        if late is not None:
            spread(*late)
        forward_last(which)
        finish(which)

    finish(CUR0)
    for s, grad, change in ((0, GRAD0, CHANGE0), (1, GRAD1, CHANGE1)):
        gradient = nn_dot(kern[s * own : (s + 1) * own, :], unpack(cur_all[s]))
        gradient = gradient - RIDGE * weights_pad[s]
        grad_all[s, slot] = pack(gradient)
        if s == 0:
            gather(grad, (0, 0), (0, 1))
        else:
            gather(grad, (1, 2), (1, 3))
        parts = nn_dot(inv_parts[s], unpack(grad_all[s]))
        delta = parts[0:own] + (parts[own : 2 * own] + parts[2 * own : 3 * own])
        change_all[s, slot] = pack(delta)
        weights_out[s] = weights_ref[s] + delta[:, :classes]
        if s == 0:
            gather(change, (0, 2), (0, 3))
        else:
            gather(change)
        current = current - nn_dot(kcol[s], unpack(change_all[s]))
        if s == 0:
            cur_all[1, slot] = pack(current)
            gather(CUR1, (1, 0), (1, 1))
    res_out[...] = current.T[0:classes, :]
    loop(1, n, feat_drain)
    for which in range(1, 7):
        drain(which)


def fused(features, residual, block_weights, block_inverse, block_columns):
    n = lax.axis_size("dp")
    groups = lax.axis_size("blk")
    shard, width = features.shape
    rows, classes = residual.shape
    own = block_weights.shape[1]
    cols = block_columns.shape[1]
    slots = n * groups
    depth = (width + 15) // 16 * 16
    place = lax.axis_index("dp") * groups + lax.axis_index("blk")
    own_columns = lax.dynamic_slice_in_dim(block_columns, place * own, own, 1).reshape(2 * own, 1)
    vmem = pl.BlockSpec(memory_space=pltpu.VMEM)
    res, weights = pl.pallas_call(
        functools.partial(fused_kernel, n),
        out_shape=(
            jax.ShapeDtypeStruct((classes, rows), F32),
            jax.ShapeDtypeStruct(block_weights.shape, F32),
        ),
        in_specs=[vmem] * 6,
        out_specs=(vmem, vmem),
        scratch_shapes=[
            pltpu.VMEM((slots, depth, rows), BF16),
            pltpu.VMEM((2, slots, rows + rows // 4, 128), BF16),
            pltpu.VMEM((2, slots, own + own // 4, 128), BF16),
            pltpu.VMEM((2, slots, own + own // 4, 128), BF16),
            pltpu.VMEM((2, 3 * own, cols), BF16),
            pltpu.VMEM((2 * own + rows, n * shard), BF16),
            pltpu.VMEM((2, rows, cols), BF16),
            pltpu.VMEM((256, rows), F32),
            pltpu.VMEM((2, own, 256), F32),
            pltpu.SemaphoreType.DMA((7, 4, n)),
            pltpu.SemaphoreType.DMA((7, 4, n)),
        ],
        compiler_params=pltpu.CompilerParams(
            collective_id=0, has_side_effects=True, vmem_limit_bytes=48 * 2**20
        ),
    )(
        features.T,
        residual.T,
        block_weights,
        jnp.swapaxes(block_inverse, 1, 2),
        own_columns,
        block_columns,
    )
    return res.T, weights


def fits(features, residual, block_weights, block_columns):
    n, groups = lax.axis_size("dp"), lax.axis_size("blk")
    shard, width = features.shape
    own, classes = block_weights.shape[1:]
    return (
        groups == 4
        and block_columns.shape[0] == 2
        and own == 64
        and residual.shape[0] == 128
        and 128 < classes <= 160
        and width % 8 == 0
        and n == 8
        and n * shard * (width + 512) <= 6 * 2**20
    )


def on_device(features, residual, block_weights, block_inverse, block_columns):
    if fits(features, residual, block_weights, block_columns):
        return fused(features, residual, block_weights, block_inverse, block_columns)
    data_count = lax.axis_size("dp")
    block_count = lax.axis_size("blk")
    data_index = lax.axis_index("dp")
    block_index = lax.axis_index("blk")
    row_count, width = features.shape
    own_count = block_weights.shape[1]
    column_count = block_columns.shape[1]
    piece_count = data_count * own_count
    gamma_rate = 4.0 / width
    frame_f = features.astype(jnp.float32)
    frame_sq = jnp.sum(frame_f * frame_f, axis=1)
    current = residual
    results = []
    for section in range(block_columns.shape[0]):
        layout = block_columns[section].reshape(data_count, block_count, own_count)
        chosen = lax.dynamic_index_in_dim(layout, block_index, 1, keepdims=False).reshape(
            piece_count
        )
        local_rows = chosen - data_index * row_count
        inside = (local_rows >= 0) & (local_rows < row_count)
        picked = jnp.take(features, jnp.clip(local_rows, 0, row_count - 1), axis=0).astype(
            jnp.float32
        )
        contrib = jnp.where(inside[:, None], picked, jnp.zeros_like(picked))
        centers = lax.psum(contrib, "dp")
        center_sq = jnp.sum(centers * centers, axis=1)
        cross = lax.dot_general(
            features,
            centers.astype(jnp.bfloat16),
            (((1,), (1,)), ((), ())),
            preferred_element_type=jnp.float32,
        )
        kernel = jnp.exp(
            -gamma_rate * (frame_sq[:, None] + center_sq[None, :] - 2.0 * cross)
        ).astype(jnp.bfloat16)
        partial_value = lax.dot_general(
            kernel,
            lax.all_gather(current.astype(jnp.bfloat16), "blk", axis=0, tiled=True),
            (((0,), (0,)), ((), ())),
            preferred_element_type=jnp.float32,
        )
        weights_own = block_weights[section]
        own_part = (
            lax.dynamic_slice_in_dim(partial_value, data_index * own_count, own_count, 0)
            - RIDGE * weights_own
        )
        partial_value = lax.dynamic_update_slice_in_dim(
            partial_value, own_part, data_index * own_count, 0
        )
        grad_piece = lax.psum(partial_value, "dp")
        stacked = lax.all_gather(grad_piece.astype(jnp.bfloat16), "blk", axis=0, tiled=True).astype(
            grad_piece.dtype
        )
        inverse = block_inverse[section].reshape(data_count, block_count, own_count, own_count)
        inverse = jnp.transpose(inverse, (1, 0, 2, 3)).reshape(column_count, own_count)
        change = lax.dot_general(
            inverse,
            stacked,
            (((0,), (0,)), ((), ())),
            precision=lax.Precision.HIGHEST,
            preferred_element_type=jnp.float32,
        )
        results.append(weights_own + change)
        change_all = lax.all_gather(change.astype(jnp.bfloat16), "dp", axis=0, tiled=True)
        current = current - lax.psum_scatter(
            jnp.dot(kernel, change_all, preferred_element_type=jnp.float32).astype(jnp.bfloat16),
            "blk",
            scatter_dimension=0,
            tiled=True,
        ).astype(jnp.float32)
    return (current, jnp.stack(results))


def solution(mesh):
    placed = (
        P("dp", None),
        P(("dp", "blk"), None),
        P(None, ("dp", "blk"), None),
        P(None, None, ("dp", "blk")),
        P(),
    )
    return jax.shard_map(
        on_device,
        mesh=mesh,
        in_specs=placed,
        out_specs=(P(("dp", "blk"), None), P(None, ("dp", "blk"), None)),
        check_vma=False,
    )
```
